32 devices in a mesh: survey: 2 (over x), sector: 16 (over z, y, core).
Axes of the slice: x: 2, y: 2, z: 4, core: 2. Of those that a mesh axis runs over, the one named last changes fastest.
Arguments:
- raw_pings: bfloat16 [32, 512, 2, 1024], P('survey', 'sector'), parts along dimension 0, may hold values from -6 to 6
- focus_matrix: bfloat16 [2, 2048, 512], replicated, may hold values from -0.25 to 0.25
- start_angle: int32 [32], P('survey'), parts along dimension 0, may hold values from 0 to 2047
- ping_count: int32 [32], P('survey'), parts along dimension 0, may hold values from 256 to 512, as said below
Outputs:
- coherence: float32 [32, 2048, 1024], P(('survey', 'sector')), parts along dimension 0
- interferogram: bfloat16 [32, 2, 2048, 1024], P(('survey', 'sector')), parts along dimension 0
The draws below stay inside these ranges and needn't reach their ends.
There are 2 independent parts, one for each index of `survey`. The reference program is written for one: setup_inputs(seed, part) draws one part's arguments, and reference() takes and returns one part's arrays. A program takes and returns all parts, laid end to end along the dimension named above; an argument that names none is the same for every part. Nothing has to cross between parts.
Inputs may be any that keep to these rules, and one draw needn't show every extreme that they name: `ping_count`: every value lies between 256 and 512, and at least one sector holds all 512 pings.
All inputs are finite; a program needn't handle non-finite values.
Results may differ from the reference program's by a relative error of at most 0.0057.
Values may be sent and summed in bfloat16 or wider, within the bound.
A program may use at most 192 MiB of HBM per device.

```python
import jax
import jax.numpy as jnp
from jax import lax

PINGS = 512
AZ = 2048
RANGES = 1024
WIN = 9
SECTORS = 16


def draw_ping_count(key, part):
    base = jax.random.fold_in(key, 7)
    first_key, second_key = jax.random.split(base)
    counts = jax.random.randint(first_key, (SECTORS,), PINGS // 2, PINGS + 1).astype(jnp.int32)
    chosen = jax.random.randint(second_key, (), 0, SECTORS)
    return counts.at[chosen].set(PINGS).astype(jnp.int32)


def touch_ends(result, own_key, low, largest):
    place = [jax.random.randint(jax.random.fold_in(own_key, axis), (), 0, length) for axis, length in enumerate(result.shape)]
    longest = result.shape.index(max(result.shape))
    neighbour = place[:longest] + [(place[longest] + 1) % result.shape[longest]] + place[longest + 1:]
    return result.at[tuple(place)].set(low).at[tuple(neighbour)].set(largest)


def levels(own_key, extent, pieces, low, top_value):
    gain = 1.0
    for position, blocks in pieces:
        heights = jax.random.uniform(jax.random.fold_in(jax.random.fold_in(own_key, 6), position), (blocks,), jnp.float32, low / len(pieces), top_value / len(pieces))
        gain = gain * jnp.repeat(jnp.exp(heights), extent[position] // blocks).reshape((-1,) + (1,) * (len(extent) - 1 - position))
    return gain


def bell_draw(stream_key, dims, deviation, reach, shards=(), kind=jnp.bfloat16):
    values = deviation * jax.random.normal(stream_key, dims, jnp.float32)
    if shards:
        values = values * levels(stream_key, dims, shards, -0.22, 0.18)
    return jnp.clip(values, -reach, reach).astype(kind)


def setup_inputs(seed: int = 0, part: int = 0) -> dict:
    keys = jax.random.split(jax.random.key(seed), 5)
    part_keys = jax.random.split(jax.random.fold_in(keys[4], part), 5)
    raw_pings = bell_draw(part_keys[0], (SECTORS, PINGS, 2, RANGES), 1.0, 6.0, ((1, 16),))
    focus_matrix = bell_draw(keys[1], (2, AZ, PINGS), PINGS ** -0.5, 0.25)
    start_angle = touch_ends(jax.random.randint(part_keys[2], (SECTORS,), 0, AZ), jax.random.fold_in(part_keys[2], 1), 0, AZ - 1).astype(jnp.int32)
    ping_count = draw_ping_count(jax.random.fold_in(jax.random.fold_in(keys[4], part), 71), part)
    return {"raw_pings": raw_pings, "focus_matrix": focus_matrix, "start_angle": start_angle, "ping_count": ping_count}


def focus_sector(raw, angle_step, valid_pings, stacked):
    pings_here = raw.shape[0]
    ranges_here = raw.shape[2]
    columns_count = stacked.shape[0] // 2
    ping_mask = (jnp.arange(pings_here, dtype=jnp.int32) < valid_pings).astype(jnp.bfloat16)
    masked = raw * ping_mask[:, None, None]
    product = jnp.dot(stacked, masked.reshape(pings_here, 2 * ranges_here), preferred_element_type=jnp.float32)
    product = product.reshape(2, columns_count, 2, ranges_here)
    real_part = product[0, :, 0] - product[1, :, 1]
    imag_part = product[0, :, 1] + product[1, :, 0]
    columns = jnp.arange(columns_count, dtype=jnp.int32)
    turn_index = angle_step * columns % columns_count
    phase_turn = 2.0 * jnp.pi / columns_count * turn_index.astype(jnp.float32)
    cosine = jnp.cos(phase_turn)[:, None]
    sine_part = jnp.sin(phase_turn)[:, None]
    mean_power = lax.optimization_barrier(jnp.mean(real_part * real_part + imag_part * imag_part, axis=0))
    inverse_rms = lax.rsqrt(mean_power + 1e-06)
    turned_real = (real_part * cosine + imag_part * sine_part) * inverse_rms
    turned_imag = (imag_part * cosine - real_part * sine_part) * inverse_rms
    return jnp.stack([turned_real, turned_imag], axis=1).astype(jnp.bfloat16)

def window_sum(field, axis, span):
    half_span = span // 2
    length_axis = field.shape[axis]
    widths = [(0, 0)] * field.ndim
    widths[axis] = (half_span, half_span)
    padded = jnp.pad(field, widths)
    total = lax.slice_in_dim(padded, 0, length_axis, axis=axis)
    for offset in range(1, span):
        total = total + lax.slice_in_dim(padded, offset, offset + length_axis, axis=axis)
    return total

def compare(own_image, other_image, span):
    f_real = own_image[:, 0].astype(jnp.float32)
    f_imag = own_image[:, 1].astype(jnp.float32)
    g_real = other_image[:, 0].astype(jnp.float32)
    g_imag = other_image[:, 1].astype(jnp.float32)
    fields = jnp.stack([f_real * g_real + f_imag * g_imag, f_imag * g_real - f_real * g_imag, f_real * f_real + f_imag * f_imag, g_real * g_real + g_imag * g_imag], axis=0)
    looked = window_sum(window_sum(fields, 1, span), 2, span)
    magnitude = jnp.sqrt(looked[0] * looked[0] + looked[1] * looked[1])
    energy = jnp.sqrt(looked[2] * looked[3] + 1e-06)
    coherence = magnitude / energy
    interferogram = (looked[0:2] / float(span * span)).astype(jnp.bfloat16)
    return (coherence, interferogram)

def reference(raw_pings, focus_matrix, start_angle, ping_count):
    stacked = focus_matrix.reshape(2 * AZ, PINGS)
    images = lax.map(lambda items: focus_sector(items[0], items[1], items[2], stacked), (raw_pings, start_angle, ping_count))
    following = jnp.roll(images, -1, axis=0)
    coherence, interferogram = lax.map(lambda pair: compare(pair[0], pair[1], WIN), (images, following))
    return (coherence, interferogram)
```

```python
import functools

import jax
import jax.numpy as jnp
from jax import lax
from jax.experimental import pallas as pl
from jax.experimental.pallas import tpu as pltpu
from jax.sharding import PartitionSpec as P

WIN = 9
ROWS = 256
HALO = 128
STRIP = 16
CHUNKS = 4


def window_start(tile, size, length):
    return min(max(tile * size - HALO, 0), length - size - 2 * HALO)


def bands(size):
    k = jnp.arange(size + 2 * HALO)[None, :, None]
    n = jnp.arange(size)[None, None, :]
    d = jnp.arange(3)[:, None, None] * HALO
    return (jnp.abs(k - d - n) <= WIN // 2).astype(jnp.bfloat16)


def focus_kernel(tiles, x_ref, h_ref, trig_ref, band_ref, s_ref, turn_ref, raw_ref, power_ref, field_ref):
    step = pl.program_id(0)
    width = s_ref.shape[2]
    length = tiles * ROWS

    @pl.when(step == 0)
    def _():
        power_ref[...] = jnp.zeros_like(power_ref)
        for image in range(2):
            turn_ref[image, :, :width] = -x_ref[image, :, width:]
            turn_ref[image, :, width:] = x_ref[image, :, :width]

    @pl.when(step < tiles)
    def _():
        rows = pl.ds(pl.multiple_of(step * ROWS, ROWS), ROWS)
        for image in range(2):
            product = jnp.dot(h_ref[0], x_ref[image], preferred_element_type=jnp.float32)
            product += jnp.dot(h_ref[1], turn_ref[image], preferred_element_type=jnp.float32)
            raw_ref[image, rows, :] = product
            square = product * product
            square = square[:, :width] + square[:, width:]
            power_ref[image] += jnp.sum(square.reshape(ROWS // 8, 8, width), axis=0)

    @pl.when((step >= tiles) & (step < 2 * tiles))
    def _():
        base = (step - tiles) * ROWS
        inverse = [
            lax.rsqrt(jnp.sum(power_ref[image], axis=0, keepdims=True) * (1.0 / length) + 1e-06)
            for image in range(2)
        ]
        for strip in range(ROWS // STRIP):
            rows = pl.ds(pl.multiple_of(base + strip * STRIP, STRIP), STRIP)
            parts = []
            for image in range(2):
                local = slice(strip * STRIP, (strip + 1) * STRIP)
                cosine = trig_ref[local, 2 * image : 2 * image + 1]
                sine = trig_ref[local, 2 * image + 1 : 2 * image + 2]
                real = raw_ref[image, rows, :width]
                imag = raw_ref[image, rows, width:]
                turned_real = (real * cosine + imag * sine) * inverse[image]
                turned_imag = (imag * cosine - real * sine) * inverse[image]
                parts.append(turned_real.astype(jnp.bfloat16).astype(jnp.float32))
                parts.append(turned_imag.astype(jnp.bfloat16).astype(jnp.float32))
            fr, fi, gr, gi = parts
            field_ref[0, rows, :] = (fr * gr + fi * gi).astype(jnp.bfloat16)
            field_ref[1, rows, :] = (fi * gr - fr * gi).astype(jnp.bfloat16)
            field_ref[2, rows, :] = (fr * fr + fi * fi).astype(jnp.bfloat16)
            field_ref[3, rows, :] = (gr * gr + gi * gi).astype(jnp.bfloat16)

    @pl.when(step > tiles)
    def _():
        tile = step - tiles - 1
        start = jnp.clip(tile * ROWS - HALO, 0, length - ROWS - 2 * HALO)
        rows = pl.ds(pl.multiple_of(start, HALO), ROWS + 2 * HALO)
        which = jnp.where(tile == 0, 0, jnp.where(tile == tiles - 1, 2, 1))
        band = band_ref[which]
        for field in range(4):
            total = jnp.dot(band, field_ref[field, rows, :], preferred_element_type=jnp.float32)
            s_ref[field] = total.astype(jnp.bfloat16)


def focus(pings, matrix, trig):
    _, depth, double = pings.shape
    width = double // 2
    length = matrix.shape[1]
    tiles = length // ROWS
    band = jnp.swapaxes(bands(ROWS), 1, 2)
    return pl.pallas_call(
        functools.partial(focus_kernel, tiles),
        grid=(2 * tiles + 1,),
        in_specs=[
            pl.BlockSpec((2, depth, double), lambda t: (0, 0, 0)),
            pl.BlockSpec((2, ROWS, depth), lambda t: (0, jnp.minimum(t, tiles - 1), 0)),
            pl.BlockSpec((ROWS, 4), lambda t: (jnp.clip(t - tiles, 0, tiles - 1), 0)),
            pl.BlockSpec(band.shape, lambda t: (0, 0, 0)),
        ],
        out_specs=pl.BlockSpec((4, ROWS, width), lambda t: (0, jnp.clip(t - tiles - 1, 0, tiles - 1), 0)),
        out_shape=jax.ShapeDtypeStruct((4, length, width), jnp.bfloat16),
        scratch_shapes=[
            pltpu.VMEM((2, depth, double), jnp.bfloat16),
            pltpu.VMEM((2, length, double), jnp.float32),
            pltpu.VMEM((2, 8, width), jnp.float32),
            pltpu.VMEM((4, length, width), jnp.bfloat16),
        ],
        compiler_params=pltpu.CompilerParams(
            dimension_semantics=("arbitrary",), vmem_limit_bytes=32 * 2**20
        ),
        cost_estimate=pl.CostEstimate(
            flops=16 * length * depth * width + 16 * length * width * ROWS,
            bytes_accessed=4 * length * depth + 8 * length * width,
            transcendentals=0,
        ),
        name="focus",
    )(pings, matrix, trig, band)


def compare_kernel(chunks, band_ref, *refs):
    s_refs, (coherence_ref, inter_ref) = refs[:chunks], refs[chunks:]
    width = s_refs[0].shape[2]
    rows = s_refs[0].shape[1]
    for part in range(chunks):
        first = window_start(part, width, width * chunks)
        band = band_ref[(part * width - first) // HALO]
        sums = []
        for field in range(4):
            pieces = []
            for chunk in range(chunks):
                low = max(first, chunk * width) - chunk * width
                high = min(first + width + 2 * HALO, (chunk + 1) * width) - chunk * width
                if high > low:
                    pieces.append(s_refs[chunk][field, :, low:high])
            block = jnp.concatenate(pieces, axis=1)
            sums.append(jnp.dot(block, band, preferred_element_type=jnp.float32))
        real, imag, own, other = sums
        lanes = slice(part * width, (part + 1) * width)
        magnitude = jnp.sqrt(real * real + imag * imag)
        coherence_ref[0, :, lanes] = magnitude * lax.rsqrt(own * other + 1e-06)
        inter_ref[0, 0, :, lanes] = (real * (1.0 / (WIN * WIN))).astype(jnp.bfloat16)
        inter_ref[0, 1, :, lanes] = (imag * (1.0 / (WIN * WIN))).astype(jnp.bfloat16)


def compare(parts):
    chunks = len(parts)
    _, length, width = parts[0].shape
    ranges = width * chunks
    band = bands(width)
    return pl.pallas_call(
        functools.partial(compare_kernel, chunks),
        grid=(length // ROWS,),
        in_specs=[pl.BlockSpec(band.shape, lambda t: (0, 0, 0))]
        + [pl.BlockSpec((4, ROWS, width), lambda t: (0, t, 0))] * chunks,
        out_specs=[
            pl.BlockSpec((1, ROWS, ranges), lambda t: (0, t, 0)),
            pl.BlockSpec((1, 2, ROWS, ranges), lambda t: (0, 0, t, 0)),
        ],
        out_shape=[
            jax.ShapeDtypeStruct((1, length, ranges), jnp.float32),
            jax.ShapeDtypeStruct((1, 2, length, ranges), jnp.bfloat16),
        ],
        compiler_params=pltpu.CompilerParams(
            dimension_semantics=("arbitrary",), vmem_limit_bytes=32 * 2**20
        ),
        cost_estimate=pl.CostEstimate(
            flops=16 * length * ranges * width, bytes_accessed=16 * length * ranges, transcendentals=0
        ),
        name="compare",
    )(band, *parts)


def turn_table(angle, length):
    index = angle * jnp.arange(length, dtype=jnp.int32) % length
    phase = 2.0 * jnp.pi / length * index.astype(jnp.float32)
    return [jnp.cos(phase), jnp.sin(phase)]


def body(raw_pings, focus_matrix, start_angle, ping_count):
    sectors = lax.axis_size("sector")
    length, depth = focus_matrix.shape[1:]
    position = lax.axis_index("sector")
    following = lax.rem(position + 1, sectors)
    route = [((i + 1) % sectors, i) for i in range(sectors)]
    trig = jnp.stack(
        turn_table(start_angle[position], length) + turn_table(start_angle[following], length), axis=1
    )
    ping = jnp.arange(depth, dtype=jnp.int32)[:, None]

    def masked(block, sector):
        flat = block.reshape(depth, -1)
        return jnp.where(ping < ping_count[sector], flat, jnp.zeros_like(flat))

    width = raw_pings.shape[3] // CHUNKS
    parts = []
    for chunk in range(CHUNKS):
        piece = raw_pings[:, :, :, chunk * width : (chunk + 1) * width]
        own = lax.all_to_all(piece, "sector", split_axis=0, concat_axis=1, tiled=True)
        other = lax.ppermute(own, "sector", route)
        pings = jnp.stack([masked(own, position), masked(other, following)])
        parts.append(focus(pings, focus_matrix, trig))
    return tuple(compare(parts))


def solution(mesh):
    return jax.shard_map(
        body,
        mesh=mesh,
        in_specs=(P("survey", "sector", None, None), P(), P("survey"), P("survey")),
        out_specs=(P(("survey", "sector"), None, None), P(("survey", "sector"), None, None, None)),
        check_vma=False,
    )
```

```python
import functools

import jax
import jax.numpy as jnp
from jax import lax
from jax.experimental import pallas as pl
from jax.experimental.pallas import tpu as pltpu
from jax.sharding import PartitionSpec as P

WIN = 9
ROWS = 256
HALO = 128
STRIP = 16
BLOCK = 512
WIDTH = 256


def window_start(tile, size, length):
    return min(max(tile * size - HALO, 0), length - size - 2 * HALO)


def bands(size):
    k = jnp.arange(size + 2 * HALO)[None, :, None]
    n = jnp.arange(size)[None, None, :]
    d = jnp.arange(3)[:, None, None] * HALO
    return (jnp.abs(k - d - n) <= WIN // 2).astype(jnp.bfloat16)


def product_step(step, blocks, x_ref, h_ref, pair_ref, raw_ref, power_ref):
    width = x_ref.shape[2]

    @pl.when(step == 0)
    def _():
        power_ref[...] = jnp.zeros_like(power_ref)
        pair_ref[0, :, :width] = x_ref[0]
        pair_ref[0, :, width:] = x_ref[1]
        pair_ref[1, :, :width] = -x_ref[1]
        pair_ref[1, :, width:] = x_ref[0]

    @pl.when(step < blocks)
    def _():
        rows = pl.ds(pl.multiple_of(step * BLOCK, BLOCK), BLOCK)
        product = jnp.dot(h_ref[0], pair_ref[0], preferred_element_type=jnp.float32)
        product += jnp.dot(h_ref[1], pair_ref[1], preferred_element_type=jnp.float32)
        raw_ref[rows, :] = product
        square = product * product
        square = square[:, :width] + square[:, width:]
        power_ref[...] += jnp.sum(square.reshape(BLOCK // 8, 8, width), axis=0)


def inverse_rms(power_ref, length):
    return lax.rsqrt(jnp.sum(power_ref[...], axis=0, keepdims=True) * (1.0 / length) + 1e-06)


def turned_strip(local, rows, trig_ref, raw_ref, inverse):
    width = inverse.shape[1]
    cosine, sine = trig_ref[local, 0:1], trig_ref[local, 1:2]
    real, imag = raw_ref[rows, :width], raw_ref[rows, width:]
    turned_real = (real * cosine + imag * sine) * inverse
    turned_imag = (imag * cosine - real * sine) * inverse
    return turned_real.astype(jnp.bfloat16), turned_imag.astype(jnp.bfloat16)


def image_kernel(blocks, x_ref, h_ref, trig_ref, image_ref, pair_ref, raw_ref, power_ref):
    step = pl.program_id(1)
    product_step(step, blocks, x_ref, h_ref, pair_ref, raw_ref, power_ref)

    @pl.when(step >= blocks)
    def _():
        base = (step - blocks) * BLOCK
        inverse = inverse_rms(power_ref, blocks * BLOCK)
        for strip in range(BLOCK // STRIP):
            rows = pl.ds(pl.multiple_of(base + strip * STRIP, STRIP), STRIP)
            local = slice(strip * STRIP, (strip + 1) * STRIP)
            real, imag = turned_strip(local, rows, trig_ref, raw_ref, inverse)
            image_ref[0, local, :] = real
            image_ref[1, local, :] = imag


def field_kernel(
    blocks, x_ref, h_ref, trig_ref, own_ref, band_ref, s_ref, pair_ref, raw_ref, power_ref, field_ref
):
    step = pl.program_id(1)
    length = blocks * BLOCK
    product_step(step, blocks, x_ref, h_ref, pair_ref, raw_ref, power_ref)

    @pl.when((step >= blocks) & (step < 2 * blocks))
    def _():
        base = (step - blocks) * BLOCK
        inverse = inverse_rms(power_ref, length)
        for strip in range(BLOCK // STRIP):
            rows = pl.ds(pl.multiple_of(base + strip * STRIP, STRIP), STRIP)
            local = slice(strip * STRIP, (strip + 1) * STRIP)
            other = turned_strip(local, rows, trig_ref, raw_ref, inverse)
            gr, gi = (value.astype(jnp.float32) for value in other)
            fr, fi = (own_ref[k, local, :].astype(jnp.float32) for k in range(2))
            field_ref[0, rows, :] = (fr * gr + fi * gi).astype(jnp.bfloat16)
            field_ref[1, rows, :] = (fi * gr - fr * gi).astype(jnp.bfloat16)
            field_ref[2, rows, :] = (fr * fr + fi * fi).astype(jnp.bfloat16)
            field_ref[3, rows, :] = (gr * gr + gi * gi).astype(jnp.bfloat16)

    @pl.when(step > blocks)
    def _():
        tiles = length // ROWS
        for part in range(BLOCK // ROWS):
            tile = (step - blocks - 1) * (BLOCK // ROWS) + part
            start = jnp.clip(tile * ROWS - HALO, 0, length - ROWS - 2 * HALO)
            rows = pl.ds(pl.multiple_of(start, HALO), ROWS + 2 * HALO)
            which = jnp.where(tile == 0, 0, jnp.where(tile == tiles - 1, 2, 1))
            band = band_ref[which]
            for field in range(4):
                total = jnp.dot(band, field_ref[field, rows, :], preferred_element_type=jnp.float32)
                s_ref[field, part * ROWS : (part + 1) * ROWS, :] = total.astype(jnp.bfloat16)


def focus(pings, matrix, trig, own=None):
    _, depth, ranges = pings.shape
    length = matrix.shape[1]
    blocks = length // BLOCK
    late = 0 if own is None else 1
    planes = 2 if own is None else 4
    in_specs = [
        pl.BlockSpec((2, depth, WIDTH), lambda j, t: (0, 0, j)),
        pl.BlockSpec((2, BLOCK, depth), lambda j, t: (0, jnp.minimum(t, blocks - 1), 0)),
        pl.BlockSpec((BLOCK, 2), lambda j, t: (jnp.clip(t - blocks, 0, blocks - 1), 0)),
    ]
    scratch = [
        pltpu.VMEM((2, depth, 2 * WIDTH), jnp.bfloat16),
        pltpu.VMEM((length, 2 * WIDTH), jnp.float32),
        pltpu.VMEM((8, WIDTH), jnp.float32),
    ]
    operands = [pings, matrix, trig]
    if own is not None:
        band = jnp.swapaxes(bands(ROWS), 1, 2)
        operands += [own, band]
        in_specs += [
            pl.BlockSpec((2, BLOCK, WIDTH), lambda j, t: (0, jnp.clip(t - blocks, 0, blocks - 1), j)),
            pl.BlockSpec(band.shape, lambda j, t: (0, 0, 0)),
        ]
        scratch.append(pltpu.VMEM((4, length, WIDTH), jnp.bfloat16))
    return pl.pallas_call(
        functools.partial(image_kernel if own is None else field_kernel, blocks),
        grid=(ranges // WIDTH, 2 * blocks + late),
        in_specs=in_specs,
        out_specs=pl.BlockSpec(
            (planes, BLOCK, WIDTH), lambda j, t: (0, jnp.clip(t - blocks - late, 0, blocks - 1), j)
        ),
        out_shape=jax.ShapeDtypeStruct((planes, length, ranges), jnp.bfloat16),
        scratch_shapes=scratch,
        compiler_params=pltpu.CompilerParams(
            dimension_semantics=("arbitrary", "arbitrary"), vmem_limit_bytes=20 * 2**20
        ),
        cost_estimate=pl.CostEstimate(
            flops=8 * length * depth * ranges + late * 16 * length * ranges * ROWS,
            bytes_accessed=4 * length * depth + 2 * planes * length * ranges,
            transcendentals=0,
        ),
        name="focus_next" if late else "focus_own",
    )(*operands)


def compare_kernel(band_ref, s_ref, coherence_ref, inter_ref):
    ranges = s_ref.shape[2]
    for part in range(ranges // WIDTH):
        first = window_start(part, WIDTH, ranges)
        band = band_ref[(part * WIDTH - first) // HALO]
        real, imag, own, other = (
            jnp.dot(
                s_ref[field, :, first : first + WIDTH + 2 * HALO], band, preferred_element_type=jnp.float32
            )
            for field in range(4)
        )
        lanes = slice(part * WIDTH, (part + 1) * WIDTH)
        magnitude = jnp.sqrt(real * real + imag * imag)
        coherence_ref[0, :, lanes] = magnitude * lax.rsqrt(own * other + 1e-06)
        inter_ref[0, 0, :, lanes] = (real * (1.0 / (WIN * WIN))).astype(jnp.bfloat16)
        inter_ref[0, 1, :, lanes] = (imag * (1.0 / (WIN * WIN))).astype(jnp.bfloat16)


def compare(sums):
    _, length, ranges = sums.shape
    band = bands(WIDTH)
    return pl.pallas_call(
        compare_kernel,
        grid=(length // ROWS,),
        in_specs=[
            pl.BlockSpec(band.shape, lambda t: (0, 0, 0)),
            pl.BlockSpec((4, ROWS, ranges), lambda t: (0, t, 0)),
        ],
        out_specs=[
            pl.BlockSpec((1, ROWS, ranges), lambda t: (0, t, 0)),
            pl.BlockSpec((1, 2, ROWS, ranges), lambda t: (0, 0, t, 0)),
        ],
        out_shape=[
            jax.ShapeDtypeStruct((1, length, ranges), jnp.float32),
            jax.ShapeDtypeStruct((1, 2, length, ranges), jnp.bfloat16),
        ],
        compiler_params=pltpu.CompilerParams(
            dimension_semantics=("arbitrary",), vmem_limit_bytes=24 * 2**20
        ),
        cost_estimate=pl.CostEstimate(
            flops=16 * length * ranges * WIDTH, bytes_accessed=16 * length * ranges, transcendentals=0
        ),
        name="compare",
    )(band, sums)


def turn_table(angle, length):
    index = angle * jnp.arange(length, dtype=jnp.int32) % length
    phase = 2.0 * jnp.pi / length * index.astype(jnp.float32)
    return jnp.stack([jnp.cos(phase), jnp.sin(phase)], axis=1)


def body(raw_pings, focus_matrix, start_angle, ping_count):
    sectors = lax.axis_size("sector")
    length, depth = focus_matrix.shape[1:]
    position = lax.axis_index("sector")
    following = lax.rem(position + 1, sectors)
    route = [((i + 1) % sectors, i) for i in range(sectors)]
    ping = jnp.arange(depth, dtype=jnp.int32)[:, None, None]

    def masked(block, sector):
        kept = jnp.where(ping < ping_count[sector], block[0], jnp.zeros_like(block[0]))
        return jnp.swapaxes(kept, 0, 1)

    own = lax.all_to_all(raw_pings, "sector", split_axis=0, concat_axis=1, tiled=True)
    other = lax.ppermute(own, "sector", route)
    image = focus(masked(own, position), focus_matrix, turn_table(start_angle[position], length))
    sums = focus(masked(other, following), focus_matrix, turn_table(start_angle[following], length), image)
    return tuple(compare(sums))


def solution(mesh):
    return jax.shard_map(
        body,
        mesh=mesh,
        in_specs=(P("survey", "sector", None, None), P(), P("survey"), P("survey")),
        out_specs=(P(("survey", "sector"), None, None), P(("survey", "sector"), None, None, None)),
        check_vma=False,
    )
```

```python
import functools

import jax
import jax.numpy as jnp
from jax import lax
from jax.experimental import pallas as pl
from jax.experimental.pallas import tpu as pltpu
from jax.sharding import PartitionSpec as P

WIN = 9
ROWS = 256
HALO = 128
STRIP = 16
BLOCK = 512
WIDTH = 256
HALVES = 2


def window_start(tile, size, length):
    return min(max(tile * size - HALO, 0), length - size - 2 * HALO)


def bands(size):
    k = jnp.arange(size + 2 * HALO)[None, :, None]
    n = jnp.arange(size)[None, None, :]
    d = jnp.arange(3)[:, None, None] * HALO
    return (jnp.abs(k - d - n) <= WIN // 2).astype(jnp.bfloat16)


def product_step(step, blocks, x_ref, h_ref, pair_ref, raw_ref, power_ref):
    width = x_ref.shape[2]

    @pl.when(step == 0)
    def _():
        power_ref[...] = jnp.zeros_like(power_ref)
        pair_ref[0, :, :width] = x_ref[0]
        pair_ref[0, :, width:] = x_ref[1]
        pair_ref[1, :, :width] = -x_ref[1]
        pair_ref[1, :, width:] = x_ref[0]

    @pl.when(step < blocks)
    def _():
        rows = pl.ds(pl.multiple_of(step * BLOCK, BLOCK), BLOCK)
        product = jnp.dot(h_ref[0], pair_ref[0], preferred_element_type=jnp.float32)
        product += jnp.dot(h_ref[1], pair_ref[1], preferred_element_type=jnp.float32)
        raw_ref[rows, :] = product
        square = product * product
        square = square[:, :width] + square[:, width:]
        power_ref[...] += jnp.sum(square.reshape(BLOCK // 8, 8, width), axis=0)


def inverse_rms(power_ref, length):
    return lax.rsqrt(jnp.sum(power_ref[...], axis=0, keepdims=True) * (1.0 / length) + 1e-06)


def turned_strip(local, rows, trig_ref, raw_ref, inverse):
    width = inverse.shape[1]
    cosine, sine = trig_ref[local, 0:1], trig_ref[local, 1:2]
    real, imag = raw_ref[rows, :width], raw_ref[rows, width:]
    turned_real = (real * cosine + imag * sine) * inverse
    turned_imag = (imag * cosine - real * sine) * inverse
    return turned_real.astype(jnp.bfloat16), turned_imag.astype(jnp.bfloat16)


def image_kernel(blocks, x_ref, h_ref, trig_ref, image_ref, pair_ref, raw_ref, power_ref):
    step = pl.program_id(1)
    product_step(step, blocks, x_ref, h_ref, pair_ref, raw_ref, power_ref)

    @pl.when(step >= blocks)
    def _():
        base = (step - blocks) * BLOCK
        inverse = inverse_rms(power_ref, blocks * BLOCK)
        for strip in range(BLOCK // STRIP):
            rows = pl.ds(pl.multiple_of(base + strip * STRIP, STRIP), STRIP)
            local = slice(strip * STRIP, (strip + 1) * STRIP)
            real, imag = turned_strip(local, rows, trig_ref, raw_ref, inverse)
            image_ref[0, local, :] = real
            image_ref[1, local, :] = imag


def field_kernel(
    blocks, x_ref, h_ref, trig_ref, own_ref, band_ref, s_ref, pair_ref, raw_ref, power_ref, field_ref
):
    step = pl.program_id(1)
    length = blocks * BLOCK
    product_step(step, blocks, x_ref, h_ref, pair_ref, raw_ref, power_ref)

    @pl.when((step >= blocks) & (step < 2 * blocks))
    def _():
        base = (step - blocks) * BLOCK
        inverse = inverse_rms(power_ref, length)
        for strip in range(BLOCK // STRIP):
            rows = pl.ds(pl.multiple_of(base + strip * STRIP, STRIP), STRIP)
            local = slice(strip * STRIP, (strip + 1) * STRIP)
            other = turned_strip(local, rows, trig_ref, raw_ref, inverse)
            gr, gi = (value.astype(jnp.float32) for value in other)
            fr, fi = (own_ref[k, local, :].astype(jnp.float32) for k in range(2))
            field_ref[0, rows, :] = (fr * gr + fi * gi).astype(jnp.bfloat16)
            field_ref[1, rows, :] = (fi * gr - fr * gi).astype(jnp.bfloat16)
            field_ref[2, rows, :] = (fr * fr + fi * fi).astype(jnp.bfloat16)
            field_ref[3, rows, :] = (gr * gr + gi * gi).astype(jnp.bfloat16)

    @pl.when(step > blocks)
    def _():
        tiles = length // ROWS
        for part in range(BLOCK // ROWS):
            tile = (step - blocks - 1) * (BLOCK // ROWS) + part
            start = jnp.clip(tile * ROWS - HALO, 0, length - ROWS - 2 * HALO)
            rows = pl.ds(pl.multiple_of(start, HALO), ROWS + 2 * HALO)
            which = jnp.where(tile == 0, 0, jnp.where(tile == tiles - 1, 2, 1))
            band = band_ref[which]
            for field in range(4):
                total = jnp.dot(band, field_ref[field, rows, :], preferred_element_type=jnp.float32)
                s_ref[field, part * ROWS : (part + 1) * ROWS, :] = total.astype(jnp.bfloat16)


def focus(pings, matrix, trig, own=None):
    _, depth, ranges = pings.shape
    length = matrix.shape[1]
    blocks = length // BLOCK
    late = 0 if own is None else 1
    planes = 2 if own is None else 4
    in_specs = [
        pl.BlockSpec((2, depth, WIDTH), lambda j, t: (0, 0, j)),
        pl.BlockSpec((2, BLOCK, depth), lambda j, t: (0, jnp.minimum(t, blocks - 1), 0)),
        pl.BlockSpec((BLOCK, 2), lambda j, t: (jnp.clip(t - blocks, 0, blocks - 1), 0)),
    ]
    scratch = [
        pltpu.VMEM((2, depth, 2 * WIDTH), jnp.bfloat16),
        pltpu.VMEM((length, 2 * WIDTH), jnp.float32),
        pltpu.VMEM((8, WIDTH), jnp.float32),
    ]
    operands = [pings, matrix, trig]
    if own is not None:
        band = jnp.swapaxes(bands(ROWS), 1, 2)
        operands += [own, band]
        in_specs += [
            pl.BlockSpec((2, BLOCK, WIDTH), lambda j, t: (0, jnp.clip(t - blocks, 0, blocks - 1), j)),
            pl.BlockSpec(band.shape, lambda j, t: (0, 0, 0)),
        ]
        scratch.append(pltpu.VMEM((4, length, WIDTH), jnp.bfloat16))
    return pl.pallas_call(
        functools.partial(image_kernel if own is None else field_kernel, blocks),
        grid=(ranges // WIDTH, 2 * blocks + late),
        in_specs=in_specs,
        out_specs=pl.BlockSpec(
            (planes, BLOCK, WIDTH), lambda j, t: (0, jnp.clip(t - blocks - late, 0, blocks - 1), j)
        ),
        out_shape=jax.ShapeDtypeStruct((planes, length, ranges), jnp.bfloat16),
        scratch_shapes=scratch,
        compiler_params=pltpu.CompilerParams(
            dimension_semantics=("arbitrary", "arbitrary"), vmem_limit_bytes=20 * 2**20
        ),
        cost_estimate=pl.CostEstimate(
            flops=8 * length * depth * ranges + late * 16 * length * ranges * ROWS,
            bytes_accessed=4 * length * depth + 2 * planes * length * ranges,
            transcendentals=0,
        ),
        name="focus_next" if late else "focus_own",
    )(*operands)


def lane_window(s_refs, field, first, size):
    width = s_refs[0].shape[2]
    pieces = []
    for index, s_ref in enumerate(s_refs):
        low = max(first - index * width, 0)
        high = min(first + size - index * width, width)
        if high > low:
            pieces.append(s_ref[field, :, low:high])
    return jnp.concatenate(pieces, axis=1) if len(pieces) > 1 else pieces[0]


def compare_kernel(band_ref, *refs):
    s_refs, (coherence_ref, inter_ref) = refs[:HALVES], refs[HALVES:]
    ranges = s_refs[0].shape[2] * HALVES
    for part in range(ranges // WIDTH):
        first = window_start(part, WIDTH, ranges)
        band = band_ref[(part * WIDTH - first) // HALO]
        real, imag, own, other = (
            jnp.dot(
                lane_window(s_refs, field, first, WIDTH + 2 * HALO), band, preferred_element_type=jnp.float32
            )
            for field in range(4)
        )
        lanes = slice(part * WIDTH, (part + 1) * WIDTH)
        magnitude = jnp.sqrt(real * real + imag * imag)
        coherence_ref[0, :, lanes] = magnitude * lax.rsqrt(own * other + 1e-06)
        inter_ref[0, 0, :, lanes] = (real * (1.0 / (WIN * WIN))).astype(jnp.bfloat16)
        inter_ref[0, 1, :, lanes] = (imag * (1.0 / (WIN * WIN))).astype(jnp.bfloat16)


def compare(sums):
    _, length, width = sums[0].shape
    ranges = width * HALVES
    band = bands(WIDTH)
    return pl.pallas_call(
        compare_kernel,
        grid=(length // ROWS,),
        in_specs=[
            pl.BlockSpec(band.shape, lambda t: (0, 0, 0)),
        ]
        + [pl.BlockSpec((4, ROWS, width), lambda t: (0, t, 0))] * HALVES,
        out_specs=[
            pl.BlockSpec((1, ROWS, ranges), lambda t: (0, t, 0)),
            pl.BlockSpec((1, 2, ROWS, ranges), lambda t: (0, 0, t, 0)),
        ],
        out_shape=[
            jax.ShapeDtypeStruct((1, length, ranges), jnp.float32),
            jax.ShapeDtypeStruct((1, 2, length, ranges), jnp.bfloat16),
        ],
        compiler_params=pltpu.CompilerParams(
            dimension_semantics=("arbitrary",), vmem_limit_bytes=24 * 2**20
        ),
        cost_estimate=pl.CostEstimate(
            flops=16 * length * ranges * WIDTH, bytes_accessed=16 * length * ranges, transcendentals=0
        ),
        name="compare",
    )(band, *sums)


def turn_table(angle, length):
    index = angle * jnp.arange(length, dtype=jnp.int32) % length
    phase = 2.0 * jnp.pi / length * index.astype(jnp.float32)
    return jnp.stack([jnp.cos(phase), jnp.sin(phase)], axis=1)


def body(raw_pings, focus_matrix, start_angle, ping_count):
    sectors = lax.axis_size("sector")
    length, depth = focus_matrix.shape[1:]
    position = lax.axis_index("sector")
    following = lax.rem(position + 1, sectors)
    route = [((i + 1) % sectors, i) for i in range(sectors)]
    ping = jnp.arange(depth, dtype=jnp.int32)[:, None, None]

    def masked(block, sector):
        kept = jnp.where(ping < ping_count[sector], block[0], jnp.zeros_like(block[0]))
        return jnp.swapaxes(kept, 0, 1)

    width = raw_pings.shape[3] // HALVES
    tables = [turn_table(start_angle[sector], length) for sector in (position, following)]
    received = []
    for half in range(HALVES):
        piece = raw_pings[:, :, :, half * width : (half + 1) * width]
        if received:
            piece, received[-1] = lax.optimization_barrier((piece, received[-1]))
        received.append(lax.all_to_all(piece, "sector", split_axis=0, concat_axis=1, tiled=True))
    sums = []
    for own in received:
        if sums:
            own, sums[-1] = lax.optimization_barrier((own, sums[-1]))
        other = lax.ppermute(own, "sector", route)
        image = focus(masked(own, position), focus_matrix, tables[0])
        sums.append(focus(masked(other, following), focus_matrix, tables[1], image))
    return tuple(compare(sums))


def solution(mesh):
    return jax.shard_map(
        body,
        mesh=mesh,
        in_specs=(P("survey", "sector", None, None), P(), P("survey"), P("survey")),
        out_specs=(P(("survey", "sector"), None, None), P(("survey", "sector"), None, None, None)),
        check_vma=False,
    )
```
